256 devices in a mesh: blk: 128 (over z, y, x), hour: 2 (over core).
Axes of the slice: x: 4, y: 4, z: 8, core: 2. Of those that a mesh axis runs over, the one named last changes fastest.
Arguments:
- spectra: bfloat16 [20480, 16, 2, 256], P('blk', 'hour'), may hold values from -600 to 600
- pair_code: int32 [128, 8], P('blk'), may hold values from 0 to 128, as said below
- pair_owner: int32 [128, 8], P('blk'), may hold values from 0 to 1, as said below
Outputs:
- stacks: float32 [128, 8, 800, 512], P('blk', 'hour')
The draws below stay inside these ranges and needn't reach their ends.
Inputs may be any that keep to these rules, and one draw needn't show every extreme that they name: `pair_code`: row b lists distinct candidates c = offset * 32 + tile with b + offset < 128; the value 128 marks an unused entry; every row lists at least one pair and row 0 lists 8. `pair_owner`: in every row each hour index appears exactly 4 times.
All inputs are finite; a program needn't handle non-finite values.
Results may differ from the reference program's by a relative error of at most 0.004.
Values may be sent and summed in bfloat16 or wider, within the bound.
No kernel may reach another device: no remote copies, remote signals or barrier semaphores. Data moves between devices by JAX's collectives and lax.ppermute only.
A program may use at most 192 MiB of HBM per device.

```python
import math
import jax
import jax.numpy as jnp
from jax import lax

F = 256
CH = 160
TILES = 32
LIST = 8
TILE = 5
CAND = 128
CAP = 4
BLOCKS = 128
CHANNELS = 20480
SEGS = 16


def pair_tables(key):
    first_key = jax.random.fold_in(key, 101)
    second_key = jax.random.fold_in(key, 102)
    third_key = jax.random.fold_in(key, 103)
    block_index = jnp.arange(BLOCKS, dtype=jnp.int32)[:, None]
    candidate = jnp.arange(CAND, dtype=jnp.int32)[None, :]
    usable = block_index + candidate // TILES < BLOCKS
    scores = jax.random.randint(first_key, (BLOCKS, CAND), 0, 1 << 20) * CAND + candidate
    scores = jnp.where(usable, scores, (1 << 29) + candidate)
    ranking = jnp.argsort(scores, axis=1, stable=True).astype(jnp.int32)
    picked_draw = jax.random.randint(second_key, (BLOCKS,), 0, LIST)
    listed_count = 1 + picked_draw * picked_draw // max(LIST - 1, 1)
    listed_count = jnp.where(jnp.arange(BLOCKS) == 0, LIST, listed_count)
    listed_count = jnp.minimum(listed_count, jnp.sum(usable.astype(jnp.int32), axis=1))
    position = jnp.arange(LIST, dtype=jnp.int32)[None, :]
    pair_codes = jnp.where(position < listed_count[:, None], ranking[:, :LIST], CAND)
    owner_scores = jax.random.randint(third_key, (BLOCKS, LIST), 0, 1 << 20) * LIST + position
    owner_order = jnp.argsort(owner_scores, axis=1, stable=True).astype(jnp.int32)
    return (pair_codes.astype(jnp.int32), (owner_order // CAP).astype(jnp.int32))


def draw_pair_code(key, part):
    return pair_tables(key)[0]


def draw_pair_owner(key, part):
    return pair_tables(key)[1]


def draw_spectra(key, part):
    scale_key = jax.random.fold_in(key, 7)
    freq_key = jax.random.fold_in(key, 8)
    noise_key = jax.random.fold_in(key, 9)
    shape = (CHANNELS, SEGS, 2, F)
    freq_scale = jnp.exp(jax.random.uniform(freq_key, (1, 1, 1, F), jnp.float32) * math.log(10.0))
    chan_scale = jnp.exp(jax.random.uniform(scale_key, (CHANNELS, SEGS, 1, 1), jnp.float32) * math.log(10.0))
    base = jnp.clip(jax.random.normal(noise_key, shape, jnp.float32), -6.0, 6.0)
    return (base * chan_scale * freq_scale).astype(jnp.bfloat16)


def setup_inputs(seed: int = 0) -> dict:
    arg_keys = jax.random.split(jax.random.key(seed), 4)
    spectra = draw_spectra(jax.random.fold_in(arg_keys[3], 71), 0)
    pair_code = draw_pair_code(jax.random.fold_in(arg_keys[3], 71), 0)
    pair_owner = draw_pair_owner(jax.random.fold_in(arg_keys[3], 71), 0)
    return dict(spectra=spectra, pair_code=pair_code, pair_owner=pair_owner)


EPSILON = 1e-06

def whiten(block_values):
    values = block_values.astype(jnp.float32)
    powers = lax.optimization_barrier(jnp.mean(values[:, :, 0, :] ** 2 + values[:, :, 1, :] ** 2, axis=-1))
    scales = lax.rsqrt(powers + EPSILON)
    return (values * scales[:, :, None, None]).astype(jnp.bfloat16)

def lag_table(freq_count, segs_all):
    lag_count = 2 * freq_count
    freq_index = jnp.arange(freq_count, dtype=jnp.int32)[:, None]
    lag_index = jnp.arange(lag_count, dtype=jnp.int32)[None, :]
    phases = 2.0 * math.pi / lag_count * (freq_index * lag_index % lag_count).astype(jnp.float32)
    weights = jnp.where(freq_index == 0, 1.0, 2.0).astype(jnp.float32) / (lag_count * math.sqrt(segs_all))
    return jnp.concatenate([weights * jnp.cos(phases), -weights * jnp.sin(phases)], axis=0)

def cross_spec(source, receiver):
    source_f = source.astype(jnp.float32)
    receiver_f = receiver.astype(jnp.float32)
    turned = jnp.stack([receiver_f[:, :, 1], -receiver_f[:, :, 0]], axis=2)
    real_part = jnp.einsum('aspf,bspf->abf', source_f, receiver_f, precision=lax.Precision.HIGHEST)
    imag_part = jnp.einsum('aspf,bspf->abf', source_f, turned, precision=lax.Precision.HIGHEST)
    return jnp.concatenate([real_part, imag_part], axis=-1)

def slot_targets(list_codes, list_owners, capacity):
    entries = list_codes.shape[0]
    listed = list_codes < CAND
    positions = jnp.arange(entries, dtype=jnp.int32)
    earlier = positions[None, :] < positions[:, None]
    same_owner = list_owners[None, :] == list_owners[:, None]
    earlier_count = lax.optimization_barrier(jnp.sum((earlier & same_owner & listed[None, :]).astype(jnp.int32), axis=1))
    return (listed, list_owners * capacity + earlier_count)

def reference(spectra, pair_code, pair_owner):
    whitened = lax.map(whiten, spectra.reshape(BLOCKS, CH, SEGS, 2, F)).reshape(CHANNELS, SEGS, 2, F)
    lag_basis = lag_table(F, SEGS)

    def block_stacks(block_index):
        list_codes = pair_code[block_index]
        list_owners = pair_owner[block_index]
        listed, target = slot_targets(list_codes, list_owners, CAP)

        def one_entry(entry_index):
            code_value = jnp.minimum(list_codes[entry_index], CAND - 1)
            offset = code_value // TILES
            tile_id = code_value % TILES
            source_start = (block_index * CH + tile_id * TILE).astype(jnp.int32)
            source = lax.dynamic_slice_in_dim(whitened, source_start, TILE, 0)
            receiver_start = (jnp.minimum(block_index + offset, BLOCKS - 1) * CH).astype(jnp.int32)
            receiver = lax.dynamic_slice_in_dim(whitened, receiver_start, CH, 0)
            spectral = cross_spec(source, receiver).reshape(TILE * CH, 2 * F)
            lagged = jnp.dot(spectral, lag_basis, precision=lax.Precision.HIGHEST)
            return jnp.where(listed[entry_index], lagged, jnp.float32(0.0))
        lagged_all = lax.map(one_entry, jnp.arange(LIST, dtype=jnp.int32))
        slot_hot = ((target[None, :] == jnp.arange(LIST, dtype=jnp.int32)[:, None]) & listed[None, :]).astype(jnp.float32)
        return jnp.einsum('se,erl->srl', slot_hot, lagged_all, precision=lax.Precision.HIGHEST)
    return lax.map(block_stacks, jnp.arange(BLOCKS, dtype=jnp.int32))
```

```python
import functools, math
import numpy as np
import jax, jax.numpy as jnp
from jax import lax
from jax.experimental import pallas as pl
from jax.experimental.pallas import tpu as pltpu
import ml_dtypes
from jax.sharding import PartitionSpec as P
EPS=1e-6
def whiten_body(x_ref, *outs, splits):
    def chunk(o_ref, base, g):
        x = x_ref[pl.ds(base + g*16, 16)].astype(jnp.float32)
        p = jnp.sum(x*x, axis=3, keepdims=True)
        p = jnp.sum(p, axis=2, keepdims=True) * (1.0/x.shape[3])
        y = x * lax.rsqrt(p + EPS)
        for s in range(x.shape[1]):
            for r in range(2):
                o_ref[s, r, pl.ds(g*16, 16)] = y[:, s, r, :].astype(jnp.bfloat16)
    base = 0
    for o_ref, n in zip(outs, splits):
        @pl.loop(0, n//16)
        def _(g, o_ref=o_ref, base=base):
            chunk(o_ref, base, pl.multiple_of(g, 1))
        base += n
def whiten(x, splits):
    c,s,_,f = x.shape
    return pl.pallas_call(functools.partial(whiten_body, splits=splits),
        out_shape=[jax.ShapeDtypeStruct((s,2,n,f), jnp.bfloat16) for n in splits],
        in_specs=[pl.BlockSpec(memory_space=pltpu.VMEM)],
        out_specs=[pl.BlockSpec(memory_space=pltpu.VMEM)]*len(splits),
        compiler_params=pltpu.CompilerParams(vmem_limit_bytes=40<<20), name="whiten")(x)

def lag_tables(F, segs):
    L = 2*F
    f = np.arange(F)[:,None]; t = np.arange(L)[None,:]
    ph = 2*np.pi/L*((f*t)%L)
    w = np.where(f==0,1.0,2.0)/(L*math.sqrt(segs))
    b = np.concatenate([w*np.cos(ph), -w*np.sin(ph)],0)
    hi = b.astype(np.float32).astype(ml_dtypes.bfloat16)
    lo = (b - hi.astype(np.float64)).astype(np.float32).astype(ml_dtypes.bfloat16)
    return jnp.asarray(hi), jnp.asarray(lo)

TILES=32; CAND=128
def slot_codes(code_ref, owner_ref, me, cap):
    n = code_ref.shape[1]
    codes = [jnp.int32(-1)]*cap
    cnt = jnp.int32(0)
    for k in range(n):
        c = code_ref[0,k]
        mine = jnp.logical_and(c < CAND, owner_ref[0,k] == me)
        for s in range(cap):
            codes[s] = jnp.where(jnp.logical_and(mine, cnt == s), c, codes[s])
        cnt = cnt + mine.astype(jnp.int32)
    return codes

def plan_body(me_ref, code_ref, owner_ref, *refs, nin, cap, tile):
    w = refs[:nin]
    src_ref, codes_ref = refs[nin:]
    codes = slot_codes(code_ref, owner_ref, me_ref[0], cap)
    for s in range(cap):
        codes_ref[s] = codes[s]
    half = nin//2
    C = sum(p.shape[2] for p in w[:half])
    row = lax.broadcasted_iota(jnp.int32, (cap*8, C), 0)
    col = lax.broadcasted_iota(jnp.int32, (cap*8, C), 1)
    target = jnp.zeros((cap*8, C), jnp.int32) - 1
    for s in range(cap):
        first = lax.rem(jnp.maximum(codes[s],0), TILES)*tile
        i = row - s*8
        target = jnp.where((i >= 0) & (i < tile), first + i, target)
    hot = jnp.where(target == col, 1.0, 0.0).astype(jnp.bfloat16)
    S = w[0].shape[0]
    for h in range(2):
        for sg in range(S):
            for r in range(2):
                acc = None; base = 0
                for p in w[h*half:(h+1)*half]:
                    n = p.shape[2]
                    d = jnp.dot(hot[:, base:base+n], p[sg, r], preferred_element_type=jnp.float32)
                    acc = d if acc is None else acc + d
                    base += n
                for s in range(cap):
                    src_ref[s, (h*S+sg)*2+r] = acc[s*8:(s+1)*8]

def plan(me, code, owner, mine, peer, cap, tile):
    S, _, _, F = mine[0].shape
    n = len(mine)*2
    smem = pl.BlockSpec(memory_space=pltpu.SMEM); vm = pl.BlockSpec(memory_space=pltpu.VMEM)
    return pl.pallas_call(functools.partial(plan_body, nin=n, cap=cap, tile=tile),
        out_shape=[jax.ShapeDtypeStruct((cap, S*4, 8, F), jnp.float32), jax.ShapeDtypeStruct((cap,), jnp.int32)],
        in_specs=[smem]*3+[vm]*n, out_specs=[vm, smem],
        compiler_params=pltpu.CompilerParams(vmem_limit_bytes=40<<20), name="plan")(me, code, owner, *mine, *peer)

def stack_body(codes_ref, src_ref, hi_ref, lo_ref, *refs, pieces, tile, cap, zero, C, passes, has_prev):
    np_ = len(pieces)
    rec = refs[:2*np_]
    k = 2*np_ + (1 if has_prev else 0)
    out_ref, xh, xl, stage, sem = refs[k:]
    F = hi_ref.shape[0]//2
    for p,(off, j0, n) in enumerate(pieces):
        rm, rp = rec[2*p], rec[2*p+1]
        S = rm.shape[0]
        @pl.loop(0, cap)
        def _(s, rm=rm, rp=rp, off=off, j0=j0, n=n, S=S):
            code = codes_ref[s]
            take = jnp.logical_and(code >= off*TILES, code < (off+1)*TILES)
            @pl.when(take)
            def _():
                @pl.loop(0, n//16)
                def _(g):
                    jj = pl.multiple_of(g*16, 16)
                    for ft in range(F//128):
                        fs = slice(ft*128, (ft+1)*128)
                        re = [jnp.zeros((16,128), jnp.float32)]*tile
                        im = [jnp.zeros((16,128), jnp.float32)]*tile
                        for h, R in enumerate((rm, rp)):
                            for sg in range(S):
                                rr = R[sg, 0, pl.ds(jj,16), fs].astype(jnp.float32)
                                ri = R[sg, 1, pl.ds(jj,16), fs].astype(jnp.float32)
                                q = (h*S+sg)*2
                                for i in range(tile):
                                    sr = src_ref[s, q, i:i+1, fs]
                                    si = src_ref[s, q+1, i:i+1, fs]
                                    re[i] = re[i] + sr*rr + si*ri
                                    im[i] = im[i] + sr*ri - si*rr
                        for i in range(tile):
                            for part, v in ((0, re[i]), (F, im[i])):
                                h16 = v.astype(jnp.bfloat16)
                                xh[i, pl.ds(jj,16), part+ft*128:part+(ft+1)*128] = h16
                                if passes > 1:
                                    xl[i, pl.ds(jj,16), part+ft*128:part+(ft+1)*128] = (v - h16.astype(jnp.float32)).astype(jnp.bfloat16)
                copies = []
                for i in range(tile):
                    a = xh[i, :n]
                    d = jnp.dot(a, hi_ref[...], preferred_element_type=jnp.float32)
                    if passes > 1:
                        d = d + jnp.dot(xl[i, :n], hi_ref[...], preferred_element_type=jnp.float32)
                        d = d + jnp.dot(a, lo_ref[...], preferred_element_type=jnp.float32)
                    stage[i, :n] = d
                    cp = pltpu.make_async_copy(stage.at[i, pl.ds(0, n)], out_ref.at[s, pl.ds(i*C + j0, n)], sem.at[i])
                    cp.start()
                    copies.append(cp)
                for cp in copies:
                    cp.wait()
    if zero:
        stage[0] = jnp.zeros(stage.shape[1:], jnp.float32)
        m = stage.shape[1]
        @pl.loop(0, cap)
        def _(s):
            @pl.when(codes_ref[s] < 0)
            def _():
                copies = [pltpu.make_async_copy(stage.at[0], out_ref.at[s, pl.ds(q*m, m)], sem.at[0]) for q in range(tile*C//m)]
                for cp in copies:
                    cp.start()
                    cp.wait()

def stack(codes, src, hi, lo, pieces, recs, prev, C, tile, cap, passes, zero=False):
    F2 = hi.shape[0]
    nmax = max(p[2] for p in pieces)
    smem = pl.BlockSpec(memory_space=pltpu.SMEM); vm = pl.BlockSpec(memory_space=pltpu.VMEM); anyb = pl.BlockSpec(memory_space=pl.ANY)
    args = [codes, src, hi, lo] + [r for pr in recs for r in pr]
    specs = [smem] + [vm]*(len(args)-1)
    alias = {}
    if prev is not None:
        alias = {len(args): 0}
        args.append(prev); specs.append(anyb)
    return pl.pallas_call(functools.partial(stack_body, pieces=pieces, tile=tile, cap=cap, zero=zero, C=C, passes=passes, has_prev=prev is not None),
        out_shape=jax.ShapeDtypeStruct((cap, tile*C, F2), jnp.float32),
        in_specs=specs, out_specs=anyb, input_output_aliases=alias,
        scratch_shapes=[pltpu.VMEM((tile, nmax, F2), jnp.bfloat16), pltpu.VMEM((tile, nmax, F2), jnp.bfloat16),
                        pltpu.VMEM((tile, nmax, F2), jnp.float32), pltpu.SemaphoreType.DMA((tile,))],
        compiler_params=pltpu.CompilerParams(vmem_limit_bytes=48<<20),
        cost_estimate=pl.CostEstimate(flops=8*10**9, bytes_accessed=8*10**6, transcendentals=0), name="stack")(*args)


SPLITS = (80, 80)


def on_device(spectra, pair_code, pair_owner):
    count = lax.axis_size("blk")
    hours = lax.axis_size("hour")
    me = lax.axis_index("hour").astype(jnp.int32).reshape(1)
    C, S, _, F = spectra.shape
    cap = pair_code.shape[1] // hours
    tile = C // TILES
    hi, lo = lag_tables(F, S * hours)

    def pull(v, steps, keep=None):
        pairs = [((d + steps) % count, d) for d in range(count) if keep is None or keep(d)]
        return lax.ppermute(v, "blk", pairs)

    def swap(v):
        return lax.ppermute(v, "hour", [(h, hours - 1 - h) for h in range(hours)])

    A, B = whiten(spectra, SPLITS)
    Ap, Bp = swap(A), swap(B)
    AN = pull(A, 4, lambda d: d % 4 == 0)
    A1 = pull(A, 1, lambda d: d % 4 != 3)
    B3 = pull(B, 3)
    BN = pull(B, 4, lambda d: d % 4 == 0)
    AW = pull(AN, -3, lambda d: d % 4 == 3)
    A1 = A1 + AW
    B1 = pull(B, 1, lambda d: d % 4 != 3)
    A3 = pull(A, 3)
    A2 = pull(A1, 1)
    B2 = pull(B3, -1)
    B1 = B1 + pull(BN, -3, lambda d: d % 4 == 3)
    source, codes = plan(me, pair_code, pair_owner, [A, B], [Ap, Bp], cap, tile)
    a, b = SPLITS

    def add(prev, pieces, recs, zero=False):
        return stack(codes, source, hi, lo, pieces, recs, prev, C, tile, cap, 3, zero)

    out = add(None, ((0, 0, a), (0, a, b)), [(A, Ap), (B, Bp)], True)
    out = add(out, ((1, 0, a),), [(A1, swap(A1))])
    out = add(out, ((3, a, b),), [(B3, swap(B3))])
    out = add(out, ((3, 0, a),), [(A3, swap(A3))])
    out = add(out, ((1, a, b),), [(B1, swap(B1))])
    out = add(out, ((2, a, b),), [(B2, swap(B2))])
    out = add(out, ((2, 0, a),), [(A2, swap(A2))])
    return out[None]


def solution(mesh):
    in_specs = (P("blk", "hour", None, None), P("blk", None), P("blk", None))
    out_specs = P("blk", "hour", None, None)
    return jax.shard_map(on_device, mesh=mesh, in_specs=in_specs, out_specs=out_specs, check_vma=False)
```

```python
import functools, math
import numpy as np
import jax, jax.numpy as jnp
from jax import lax
from jax.experimental import pallas as pl
from jax.experimental.pallas import tpu as pltpu
import ml_dtypes
from jax.sharding import PartitionSpec as P
PARTS = 1
EPS = 1e-6
TILES = 32
CAND = 128


def planes(x_ref, base, put, n):
    segs, parts, freq = x_ref.shape[1:]

    @pl.loop(0, n//16)
    def _(g):
        rows = pl.ds(pl.multiple_of(base + g*16, 16), 16)
        x = x_ref[rows].astype(jnp.float32).reshape(16, segs*parts, freq)
        x = jnp.swapaxes(x, 0, 1)
        for sg in range(segs):
            re, im = x[2*sg], x[2*sg+1]
            power = jnp.sum(re*re + im*im, axis=1, keepdims=True)*(1.0/freq)
            scale = lax.rsqrt(power + EPS)
            put(sg, 0, g, (re*scale).astype(jnp.bfloat16))
            put(sg, 1, g, (im*scale).astype(jnp.bfloat16))


def own_body(me_ref, x_ref, *outs):
    n = outs[0].shape[2]
    for k, o_ref in enumerate(outs):
        def put(sg, r, g, v, o_ref=o_ref):
            o_ref[sg, r, pl.ds(pl.multiple_of(g*16, 16), 16)] = v
        planes(x_ref, lax.rem(me_ref[0] + k, 2)*n, put, n)


def join_body(me_ref, x_ref, own_ref, o_ref, *, k):
    S, _, n, _ = own_ref.shape
    mine = me_ref[0]*S
    theirs = (1 - me_ref[0])*S
    for sg in range(S):
        for r in range(2):
            o_ref[mine + sg, r] = own_ref[sg, r]
    def put(sg, r, g, v):
        o_ref[theirs + sg, r, pl.ds(pl.multiple_of(g*16, 16), 16)] = v
    planes(x_ref, lax.rem(me_ref[0] + k, 2)*n, put, n)


SMEM = pl.BlockSpec(memory_space=pltpu.SMEM)
VMEM = pl.BlockSpec(memory_space=pltpu.VMEM)


def whiten_own(me, x):
    c, s, _, f = x.shape
    half = jax.ShapeDtypeStruct((s, 2, c//2, f), jnp.bfloat16)
    return pl.pallas_call(own_body, out_shape=[half, half], in_specs=[SMEM, VMEM], out_specs=[VMEM, VMEM],
        compiler_params=pltpu.CompilerParams(vmem_limit_bytes=40<<20),
        cost_estimate=pl.CostEstimate(flops=10**7, bytes_accessed=12*10**6, transcendentals=0), name="whiten_own")(me, x)


def whiten_join(me, x, own, k):
    s, _, n, f = own.shape
    return pl.pallas_call(functools.partial(join_body, k=k), out_shape=jax.ShapeDtypeStruct((2*s, 2, n, f), jnp.bfloat16),
        in_specs=[SMEM, VMEM, VMEM], out_specs=VMEM,
        compiler_params=pltpu.CompilerParams(vmem_limit_bytes=40<<20),
        cost_estimate=pl.CostEstimate(flops=10**7, bytes_accessed=7*10**6, transcendentals=0), name="whiten_join")(me, x, own)


def lag_basis(F, segs, parts):
    L = 2*F
    f = np.arange(F)[:,None]; t = np.arange(L)[None,:]
    ph = 2*np.pi/L*((f*t)%L)
    w = np.where(f==0,1.0,2.0)/(L*math.sqrt(segs))
    b = np.concatenate([w*np.cos(ph), -w*np.sin(ph)],0)
    hi = b.astype(np.float32).astype(ml_dtypes.bfloat16)
    lo = (b - hi.astype(np.float64)).astype(np.float32).astype(ml_dtypes.bfloat16)
    return jnp.asarray(np.concatenate([hi, hi, lo][:parts], 0))

def slot_codes(code_ref, owner_ref, me, cap):
    n = code_ref.shape[1]
    codes = [jnp.int32(-1)]*cap
    cnt = jnp.int32(0)
    for k in range(n):
        c = code_ref[0,k]
        mine = jnp.logical_and(c < CAND, owner_ref[0,k] == me)
        for s in range(cap):
            codes[s] = jnp.where(jnp.logical_and(mine, cnt == s), c, codes[s])
        cnt = cnt + mine.astype(jnp.int32)
    return codes

def plan_body(me_ref, code_ref, owner_ref, first_ref, second_ref, src_ref, codes_ref, *, cap, tile):
    codes = slot_codes(code_ref, owner_ref, me_ref[0], cap)
    for s in range(cap):
        codes_ref[s] = codes[s]
    S, _, n, _ = first_ref.shape
    row = lax.broadcasted_iota(jnp.int32, (cap*8, n), 0)
    col = lax.broadcasted_iota(jnp.int32, (cap*8, n), 1)
    target = jnp.zeros((cap*8, n), jnp.int32) - 1
    for s in range(cap):
        start = lax.rem(jnp.maximum(codes[s], 0), TILES)*tile
        i = row - s*8
        target = jnp.where((i >= 0) & (i < tile), start + i, target)
    hots = []
    for k in range(2):
        base = lax.rem(me_ref[0] + k, 2)*n
        hots.append(jnp.where(target == col + base, 1.0, 0.0).astype(jnp.bfloat16))
    for sg in range(S):
        picked = []
        for r in range(2):
            picked.append(sum(jnp.dot(hot, p[sg, r], preferred_element_type=jnp.float32)
                              for hot, p in zip(hots, (first_ref, second_ref))))
        sr, si = picked
        for q, v in enumerate((sr, sr + si, sr - si)):
            for s in range(cap):
                src_ref[s, sg*3+q] = v[s*8:(s+1)*8]


def plan(me, code, owner, first, second, cap, tile):
    S, _, _, F = first.shape
    return pl.pallas_call(functools.partial(plan_body, cap=cap, tile=tile),
        out_shape=[jax.ShapeDtypeStruct((cap, S*3, 8, F), jnp.float32), jax.ShapeDtypeStruct((cap,), jnp.int32)],
        in_specs=[SMEM]*3+[VMEM]*2, out_specs=[VMEM, SMEM],
        compiler_params=pltpu.CompilerParams(vmem_limit_bytes=40<<20),
        cost_estimate=pl.CostEstimate(flops=10**8, bytes_accessed=4*10**6, transcendentals=0), name="plan")(me, code, owner, first, second)


def stack_body(me_ref, codes_ref, src_ref, basis_ref, *refs, pieces, tile, cap, zero, C, has_prev):
    count = len(pieces)
    rec = refs[:count]
    out_ref, x_ref, stage, used, sem = refs[count + (1 if has_prev else 0):]
    F2 = basis_ref.shape[1]
    F = F2//2
    parts = basis_ref.shape[0]//F2
    used[0] = 0
    part = stage.shape[1]//tile

    def drain(b):
        for i in range(tile):
            pltpu.make_async_copy(stage.at[b, pl.ds(0, part)], out_ref.at[0, pl.ds(0, part)], sem.at[b, i]).wait()

    if zero:
        m = 160
        stage[0, :m] = jnp.zeros((m, F2), jnp.float32)
        @pl.loop(0, cap)
        def _(s):
            @pl.when(codes_ref[s] < 0)
            def _():
                copies = [pltpu.make_async_copy(stage.at[0, pl.ds(0, m)], out_ref.at[s, pl.ds(i*m, m)], sem.at[0, i]) for i in range(tile*C//m)]
                for cp in copies:
                    cp.start()
                for cp in copies:
                    cp.wait()

    for R, (one, two) in zip(rec, pieces):
        S, _, n, _ = R.shape
        off = jnp.where(me_ref[0] == 0, one[0], two[0])
        j0 = jnp.where(me_ref[0] == 0, one[1], two[1])*n
        @pl.loop(0, cap)
        def _(s, R=R, off=off, j0=j0, n=n, S=S):
            code = codes_ref[s]
            take = jnp.logical_and(code >= off*TILES, code < (off+1)*TILES)
            @pl.when(take)
            def _():
                @pl.loop(0, n//16)
                def _(g):
                    jj = pl.multiple_of(g*16, 16)
                    for ft in range(F//128):
                        fs = slice(ft*128, (ft+1)*128)
                        k1 = [jnp.zeros((16, 128), jnp.float32)]*tile
                        k2 = list(k1)
                        k3 = list(k1)
                        for sg in range(S):
                            rr = R[sg, 0, pl.ds(jj, 16), fs].astype(jnp.float32)
                            ri = R[sg, 1, pl.ds(jj, 16), fs].astype(jnp.float32)
                            both = rr + ri
                            q = sg*3
                            for i in range(tile):
                                k1[i] = k1[i] + src_ref[s, q, i:i+1, fs]*both
                                k2[i] = k2[i] + src_ref[s, q+1, i:i+1, fs]*rr
                                k3[i] = k3[i] + src_ref[s, q+2, i:i+1, fs]*ri
                        for i in range(tile):
                            for base, v in ((0, k1[i]-k3[i]), (F, k1[i]-k2[i])):
                                lo = base + ft*128
                                top = v.astype(jnp.bfloat16)
                                rows = pl.ds(pl.multiple_of(i*n + jj, 16), 16)
                                x_ref[rows, lo:lo+128] = top
                                if parts > 1:
                                    x_ref[rows, F2+lo:F2+lo+128] = (v - top.astype(jnp.float32)).astype(jnp.bfloat16)
                                if parts > 2:
                                    x_ref[rows, 2*F2+lo:2*F2+lo+128] = top
                b = lax.rem(used[0], 2)
                @pl.when(used[0] >= 2)
                def _():
                    drain(b)
                stage[b] = jnp.dot(x_ref[...], basis_ref[...], preferred_element_type=jnp.float32)
                for i in range(tile):
                    pltpu.make_async_copy(stage.at[b, pl.ds(i*n, n)], out_ref.at[s, pl.ds(pl.multiple_of(i*C + j0, 16), n)], sem.at[b, i]).start()
                used[0] = used[0] + 1

    for back in (1, 2):
        @pl.when(used[0] >= back)
        def _(back=back):
            drain(lax.rem(used[0] - back, 2))


def stack(me, codes, src, basis, pieces, recs, prev, C, tile, cap, zero=False):
    K, F2 = basis.shape
    rows = tile*recs[0].shape[2]
    hbm = pl.BlockSpec(memory_space=pl.ANY)
    args = [me, codes, src, basis] + recs
    specs = [SMEM, SMEM] + [VMEM]*(len(args)-2)
    alias = {}
    if prev is not None:
        alias = {len(args): 0}
        args.append(prev)
        specs.append(hbm)
    return pl.pallas_call(functools.partial(stack_body, pieces=pieces, tile=tile, cap=cap, zero=zero, C=C, has_prev=prev is not None),
        out_shape=jax.ShapeDtypeStruct((cap, tile*C, F2), jnp.float32),
        in_specs=specs, out_specs=hbm, input_output_aliases=alias,
        scratch_shapes=[pltpu.VMEM((rows, K), jnp.bfloat16), pltpu.VMEM((2, rows, F2), jnp.float32), pltpu.SMEM((1,), jnp.int32), pltpu.SemaphoreType.DMA((2, tile))],
        compiler_params=pltpu.CompilerParams(vmem_limit_bytes=40<<20),
        cost_estimate=pl.CostEstimate(flops=10**8, bytes_accessed=10**6, transcendentals=0), name="stack")(*args)


def on_device(spectra, pair_code, pair_owner):
    count = lax.axis_size("blk")
    hours = lax.axis_size("hour")
    me = lax.axis_index("hour").astype(jnp.int32).reshape(1)
    C, S, _, F = spectra.shape
    cap = pair_code.shape[1] // hours
    tile = C // TILES
    basis = lag_basis(F, S * hours, PARTS)

    def pull(v, zero, one):
        pairs = []
        for h, source in enumerate((zero, one)):
            for d in range(count):
                at = source(d)
                if at is not None:
                    pairs.append(((at % count) * hours + h, d * hours + h))
        return lax.ppermute(v, ("blk", "hour"), pairs)

    def swap(v):
        return lax.ppermute(v, "hour", [(h, hours - 1 - h) for h in range(hours)])

    def none(d):
        return None

    def x_of(d):
        return d % 4

    def y_ring(d):
        return (d // 16) * 16 + (d + 4) % 16 if x_of(d) == 0 else None

    def last_column(d):
        if x_of(d) != 3:
            return None
        return d + 13 if (d // 4) % 4 == 3 else d - 3

    def ahead(d):
        return d + 1 if x_of(d) != 3 else None

    peer = swap(spectra)
    own1, own2 = whiten_own(me, spectra)
    first = whiten_join(me, peer, own1, 0)
    near1 = pull(first, y_ring, none)
    got1 = pull(first, ahead, lambda d: d + 3)
    second = whiten_join(me, peer, own2, 1)
    near2 = pull(second, y_ring, none)
    wrap1 = pull(near1, last_column, none)
    got2 = pull(second, ahead, lambda d: d + 3)
    got1 = got1 + wrap1
    got3 = pull(got1, lambda d: d + 1, lambda d: d - 1)
    wrap2 = pull(near2, last_column, none)
    got2 = got2 + wrap2
    source, codes = plan(me, pair_code, pair_owner, first, second, cap, tile)
    swap1 = swap(got1)

    def add(prev, pieces, recs, zero=False):
        return stack(me, codes, source, basis, pieces, recs, prev, C, tile, cap, zero)

    out = add(None, (((0, 0), (0, 1)), ((0, 1), (0, 0))), [first, second], True)
    out = add(out, (((1, 0), (3, 1)), ((3, 1), (1, 0))), [got1, swap1])
    got2, out = lax.optimization_barrier((got2, out))
    swap2 = swap(got2)
    got3, out = lax.optimization_barrier((got3, out))
    swap3 = swap(got3)
    out = add(out, (((1, 1), (3, 0)), ((3, 0), (1, 1))), [got2, swap2])
    out = add(out, (((2, 0), (2, 1)), ((2, 1), (2, 0))), [got3, swap3])
    return out[None]


def solution(mesh):
    in_specs = (P("blk", "hour", None, None), P("blk", None), P("blk", None))
    out_specs = P("blk", "hour", None, None)
    return jax.shard_map(on_device, mesh=mesh, in_specs=in_specs, out_specs=out_specs, check_vma=False)
```

```python
import functools, math
import numpy as np
import jax, jax.numpy as jnp
from jax import lax
from jax.experimental import pallas as pl
from jax.experimental.pallas import tpu as pltpu
import ml_dtypes
from jax.sharding import PartitionSpec as P
PARTS = 1
EPS = 1e-6
TILES = 32
CAND = 128


def planes(x_ref, base, put, n):
    segs, parts, freq = x_ref.shape[1:]

    @pl.loop(0, n//16)
    def _(g):
        rows = pl.ds(pl.multiple_of(base + g*16, 16), 16)
        x = x_ref[rows].astype(jnp.float32).reshape(16, segs*parts, freq)
        x = jnp.swapaxes(x, 0, 1)
        for sg in range(segs):
            re, im = x[2*sg], x[2*sg+1]
            power = jnp.sum(re*re + im*im, axis=1, keepdims=True)*(1.0/freq)
            scale = lax.rsqrt(power + EPS)
            put(sg, 0, g, (re*scale).astype(jnp.bfloat16))
            put(sg, 1, g, (im*scale).astype(jnp.bfloat16))


def own_body(me_ref, x_ref, *outs):
    n = outs[0].shape[2]
    for k, o_ref in enumerate(outs):
        def put(sg, r, g, v, o_ref=o_ref):
            o_ref[sg, r, pl.ds(pl.multiple_of(g*16, 16), 16)] = v
        planes(x_ref, lax.rem(me_ref[0] + k, 2)*n, put, n)


def join_body(me_ref, x_ref, own_ref, o_ref, *, k):
    S, _, n, _ = own_ref.shape
    mine = me_ref[0]*S
    theirs = (1 - me_ref[0])*S
    for sg in range(S):
        for r in range(2):
            o_ref[mine + sg, r] = own_ref[sg, r]
    def put(sg, r, g, v):
        o_ref[theirs + sg, r, pl.ds(pl.multiple_of(g*16, 16), 16)] = v
    planes(x_ref, lax.rem(me_ref[0] + k, 2)*n, put, n)


SMEM = pl.BlockSpec(memory_space=pltpu.SMEM)
VMEM = pl.BlockSpec(memory_space=pltpu.VMEM)


def whiten_own(me, x):
    c, s, _, f = x.shape
    half = jax.ShapeDtypeStruct((s, 2, c//2, f), jnp.bfloat16)
    return pl.pallas_call(own_body, out_shape=[half, half], in_specs=[SMEM, VMEM], out_specs=[VMEM, VMEM],
        compiler_params=pltpu.CompilerParams(vmem_limit_bytes=18<<20),
        cost_estimate=pl.CostEstimate(flops=10**7, bytes_accessed=12*10**6, transcendentals=0), name="whiten_own")(me, x)


def whiten_join(me, x, own, k):
    s, _, n, f = own.shape
    return pl.pallas_call(functools.partial(join_body, k=k), out_shape=jax.ShapeDtypeStruct((2*s, 2, n, f), jnp.bfloat16),
        in_specs=[SMEM, VMEM, VMEM], out_specs=VMEM,
        compiler_params=pltpu.CompilerParams(vmem_limit_bytes=18<<20),
        cost_estimate=pl.CostEstimate(flops=10**7, bytes_accessed=7*10**6, transcendentals=0), name="whiten_join")(me, x, own)


def lag_basis(F, segs, parts):
    L = 2*F
    f = np.arange(F)[:,None]; t = np.arange(L)[None,:]
    ph = 2*np.pi/L*((f*t)%L)
    w = np.where(f==0,1.0,2.0)/(L*math.sqrt(segs))
    b = np.concatenate([w*np.cos(ph), -w*np.sin(ph)],0)
    hi = b.astype(np.float32).astype(ml_dtypes.bfloat16)
    lo = (b - hi.astype(np.float64)).astype(np.float32).astype(ml_dtypes.bfloat16)
    return jnp.asarray(np.concatenate([hi, hi, lo][:parts], 0))

def slot_codes(code_ref, owner_ref, me, cap):
    n = code_ref.shape[1]
    codes = [jnp.int32(-1)]*cap
    cnt = jnp.int32(0)
    for k in range(n):
        c = code_ref[0,k]
        mine = jnp.logical_and(c < CAND, owner_ref[0,k] == me)
        for s in range(cap):
            codes[s] = jnp.where(jnp.logical_and(mine, cnt == s), c, codes[s])
        cnt = cnt + mine.astype(jnp.int32)
    return codes

def plan_body(me_ref, code_ref, owner_ref, first_ref, second_ref, src_ref, codes_ref, *, cap, tile):
    codes = slot_codes(code_ref, owner_ref, me_ref[0], cap)
    for s in range(cap):
        codes_ref[s] = codes[s]
    S, _, n, _ = first_ref.shape
    row = lax.broadcasted_iota(jnp.int32, (cap*8, n), 0)
    col = lax.broadcasted_iota(jnp.int32, (cap*8, n), 1)
    target = jnp.zeros((cap*8, n), jnp.int32) - 1
    for s in range(cap):
        start = lax.rem(jnp.maximum(codes[s], 0), TILES)*tile
        i = row - s*8
        target = jnp.where((i >= 0) & (i < tile), start + i, target)
    hots = []
    for k in range(2):
        base = lax.rem(me_ref[0] + k, 2)*n
        hots.append(jnp.where(target == col + base, 1.0, 0.0).astype(jnp.bfloat16))
    for sg in range(S):
        picked = []
        for r in range(2):
            picked.append(sum(jnp.dot(hot, p[sg, r], preferred_element_type=jnp.float32)
                              for hot, p in zip(hots, (first_ref, second_ref))))
        sr, si = picked
        for q, v in enumerate((sr, sr + si, sr - si)):
            for s in range(cap):
                src_ref[s, sg*3+q] = v[s*8:(s+1)*8]


def plan(me, code, owner, first, second, cap, tile):
    S, _, _, F = first.shape
    return pl.pallas_call(functools.partial(plan_body, cap=cap, tile=tile),
        out_shape=[jax.ShapeDtypeStruct((cap, S*3, 8, F), jnp.float32), jax.ShapeDtypeStruct((cap,), jnp.int32)],
        in_specs=[SMEM]*3+[VMEM]*2, out_specs=[VMEM, SMEM],
        compiler_params=pltpu.CompilerParams(vmem_limit_bytes=18<<20),
        cost_estimate=pl.CostEstimate(flops=10**8, bytes_accessed=4*10**6, transcendentals=0), name="plan")(me, code, owner, first, second)


def stack_body(me_ref, codes_ref, src_ref, basis_ref, *refs, pieces, tile, cap, zero, C, has_prev):
    count = len(pieces)
    rec = refs[:count]
    out_ref, x_ref, stage, used, sem = refs[count + (1 if has_prev else 0):]
    F2 = basis_ref.shape[1]
    F = F2//2
    parts = basis_ref.shape[0]//F2
    used[0] = 0
    part = stage.shape[1]//tile

    def drain(b):
        for i in range(tile):
            pltpu.make_async_copy(stage.at[b, pl.ds(0, part)], out_ref.at[0, pl.ds(0, part)], sem.at[b, i]).wait()

    if zero:
        m = 160
        stage[0, :m] = jnp.zeros((m, F2), jnp.float32)
        @pl.loop(0, cap)
        def _(s):
            @pl.when(codes_ref[s] < 0)
            def _():
                copies = [pltpu.make_async_copy(stage.at[0, pl.ds(0, m)], out_ref.at[s, pl.ds(i*m, m)], sem.at[0, i]) for i in range(tile*C//m)]
                for cp in copies:
                    cp.start()
                for cp in copies:
                    cp.wait()

    for R, (one, two) in zip(rec, pieces):
        S, _, n, _ = R.shape
        off = jnp.where(me_ref[0] == 0, one[0], two[0])
        j0 = jnp.where(me_ref[0] == 0, one[1], two[1])*n
        @pl.loop(0, cap)
        def _(s, R=R, off=off, j0=j0, n=n, S=S):
            code = codes_ref[s]
            take = jnp.logical_and(code >= off*TILES, code < (off+1)*TILES)
            @pl.when(take)
            def _():
                @pl.loop(0, n//16)
                def _(g):
                    jj = pl.multiple_of(g*16, 16)
                    for ft in range(F//128):
                        fs = slice(ft*128, (ft+1)*128)
                        k1 = [jnp.zeros((16, 128), jnp.float32)]*tile
                        k2 = list(k1)
                        k3 = list(k1)
                        for sg in range(S):
                            rr = R[sg, 0, pl.ds(jj, 16), fs].astype(jnp.float32)
                            ri = R[sg, 1, pl.ds(jj, 16), fs].astype(jnp.float32)
                            both = rr + ri
                            q = sg*3
                            for i in range(tile):
                                k1[i] = k1[i] + src_ref[s, q, i:i+1, fs]*both
                                k2[i] = k2[i] + src_ref[s, q+1, i:i+1, fs]*rr
                                k3[i] = k3[i] + src_ref[s, q+2, i:i+1, fs]*ri
                        for i in range(tile):
                            for base, v in ((0, k1[i]-k3[i]), (F, k1[i]-k2[i])):
                                lo = base + ft*128
                                top = v.astype(jnp.bfloat16)
                                rows = pl.ds(pl.multiple_of(i*n + jj, 16), 16)
                                x_ref[rows, lo:lo+128] = top
                                if parts > 1:
                                    x_ref[rows, F2+lo:F2+lo+128] = (v - top.astype(jnp.float32)).astype(jnp.bfloat16)
                                if parts > 2:
                                    x_ref[rows, 2*F2+lo:2*F2+lo+128] = top
                b = lax.rem(used[0], 2)
                @pl.when(used[0] >= 2)
                def _():
                    drain(b)
                stage[b] = jnp.dot(x_ref[...], basis_ref[...], preferred_element_type=jnp.float32)
                for i in range(tile):
                    pltpu.make_async_copy(stage.at[b, pl.ds(i*n, n)], out_ref.at[s, pl.ds(pl.multiple_of(i*C + j0, 16), n)], sem.at[b, i]).start()
                used[0] = used[0] + 1

    for back in (1, 2):
        @pl.when(used[0] >= back)
        def _(back=back):
            drain(lax.rem(used[0] - back, 2))


def stack(me, codes, src, basis, pieces, recs, prev, C, tile, cap, zero=False):
    K, F2 = basis.shape
    rows = tile*recs[0].shape[2]
    hbm = pl.BlockSpec(memory_space=pl.ANY)
    args = [me, codes, src, basis] + recs
    specs = [SMEM, SMEM] + [VMEM]*(len(args)-2)
    alias = {}
    if prev is not None:
        alias = {len(args): 0}
        args.append(prev)
        specs.append(hbm)
    return pl.pallas_call(functools.partial(stack_body, pieces=pieces, tile=tile, cap=cap, zero=zero, C=C, has_prev=prev is not None),
        out_shape=jax.ShapeDtypeStruct((cap, tile*C, F2), jnp.float32),
        in_specs=specs, out_specs=hbm, input_output_aliases=alias,
        scratch_shapes=[pltpu.VMEM((rows, K), jnp.bfloat16), pltpu.VMEM((2, rows, F2), jnp.float32), pltpu.SMEM((1,), jnp.int32), pltpu.SemaphoreType.DMA((2, tile))],
        compiler_params=pltpu.CompilerParams(vmem_limit_bytes=18<<20),
        cost_estimate=pl.CostEstimate(flops=10**8, bytes_accessed=10**6, transcendentals=0), name="stack")(*args)


def on_device(spectra, pair_code, pair_owner):
    count = lax.axis_size("blk")
    hours = lax.axis_size("hour")
    me = lax.axis_index("hour").astype(jnp.int32).reshape(1)
    C, S, _, F = spectra.shape
    cap = pair_code.shape[1] // hours
    tile = C // TILES
    basis = lag_basis(F, S * hours, PARTS)

    def pull(v, zero, one):
        pairs = []
        for h, source in enumerate((zero, one)):
            for d in range(count):
                at = source(d)
                if at is not None:
                    pairs.append(((at % count) * hours + h, d * hours + h))
        return lax.ppermute(v, ("blk", "hour"), pairs)

    def swap(v):
        return lax.ppermute(v, "hour", [(h, hours - 1 - h) for h in range(hours)])

    def none(d):
        return None

    def x_of(d):
        return d % 4

    def y_ring(d):
        return (d // 16) * 16 + (d + 4) % 16 if x_of(d) == 0 else None

    def last_column(d):
        if x_of(d) != 3:
            return None
        return d + 13 if (d // 4) % 4 == 3 else d - 3

    def ahead(d):
        return d + 1 if x_of(d) != 3 else None

    peer = swap(spectra)
    own1, own2 = whiten_own(me, spectra)
    first = whiten_join(me, peer, own1, 0)
    near1 = pull(first, y_ring, none)
    got1 = pull(first, ahead, lambda d: d + 3)
    second = whiten_join(me, peer, own2, 1)
    near2 = pull(second, y_ring, none)
    wrap1 = pull(near1, last_column, none)
    got2 = pull(second, ahead, lambda d: d + 3)
    got1 = got1 + wrap1
    got3 = pull(got1, lambda d: d + 1, lambda d: d - 1)
    wrap2 = pull(near2, last_column, none)
    source, codes = plan(me, pair_code, pair_owner, first, second, cap, tile)
    swap1 = swap(got1)

    def add(prev, pieces, recs, zero=False):
        return stack(me, codes, source, basis, pieces, recs, prev, C, tile, cap, zero)

    out = add(None, (((0, 0), (0, 1)), ((0, 1), (0, 0)), ((1, 0), (3, 1))), [first, second, got1], True)
    got2, wrap2, out = lax.optimization_barrier((got2, wrap2, out))
    got2 = got2 + wrap2
    swap2 = swap(got2)
    out = add(out, (((3, 1), (1, 0)), ((1, 1), (3, 0))), [swap1, got2])
    got3, out = lax.optimization_barrier((got3, out))
    swap3 = swap(got3)
    out = add(out, (((3, 0), (1, 1)), ((2, 0), (2, 1))), [swap2, got3])
    out = add(out, (((2, 1), (2, 0)),), [swap3])
    return out[None]


def solution(mesh):
    in_specs = (P("blk", "hour", None, None), P("blk", None), P("blk", None))
    out_specs = P("blk", "hour", None, None)
    return jax.shard_map(on_device, mesh=mesh, in_specs=in_specs, out_specs=out_specs, check_vma=False)
```

```python
import functools, math
import numpy as np
import jax, jax.numpy as jnp
from jax import lax
from jax.experimental import pallas as pl
from jax.experimental.pallas import tpu as pltpu
import ml_dtypes
from jax.sharding import PartitionSpec as P
PARTS = 1
EPS = 1e-6
TILES = 32
CAND = 128


def planes(x_ref, base, put, n):
    segs, parts, freq = x_ref.shape[1:]

    @pl.loop(0, n//16)
    def _(g):
        rows = pl.ds(pl.multiple_of(base + g*16, 16), 16)
        x = x_ref[rows].astype(jnp.float32).reshape(16, segs*parts, freq)
        x = jnp.swapaxes(x, 0, 1)
        for sg in range(segs):
            re, im = x[2*sg], x[2*sg+1]
            power = jnp.sum(re*re + im*im, axis=1, keepdims=True)*(1.0/freq)
            scale = lax.rsqrt(power + EPS)
            put(sg, 0, g, (re*scale).astype(jnp.bfloat16))
            put(sg, 1, g, (im*scale).astype(jnp.bfloat16))


def own_body(me_ref, x_ref, *outs):
    n = outs[0].shape[2]
    for k, o_ref in enumerate(outs):
        def put(sg, r, g, v, o_ref=o_ref):
            o_ref[sg, r, pl.ds(pl.multiple_of(g*16, 16), 16)] = v
        planes(x_ref, lax.rem(me_ref[0] + k, 2)*n, put, n)


def join_body(me_ref, x_ref, own_ref, o_ref, *, k):
    S, _, n, _ = own_ref.shape
    mine = me_ref[0]*S
    theirs = (1 - me_ref[0])*S
    for sg in range(S):
        for r in range(2):
            o_ref[mine + sg, r] = own_ref[sg, r]
    def put(sg, r, g, v):
        o_ref[theirs + sg, r, pl.ds(pl.multiple_of(g*16, 16), 16)] = v
    planes(x_ref, lax.rem(me_ref[0] + k, 2)*n, put, n)


SMEM = pl.BlockSpec(memory_space=pltpu.SMEM)
VMEM = pl.BlockSpec(memory_space=pltpu.VMEM)


def whiten_own(me, x):
    c, s, _, f = x.shape
    half = jax.ShapeDtypeStruct((s, 2, c//2, f), jnp.bfloat16)
    return pl.pallas_call(own_body, out_shape=[half, half], in_specs=[SMEM, VMEM], out_specs=[VMEM, VMEM],
        compiler_params=pltpu.CompilerParams(vmem_limit_bytes=18<<20),
        cost_estimate=pl.CostEstimate(flops=10**7, bytes_accessed=12*10**6, transcendentals=0), name="whiten_own")(me, x)


def whiten_join(me, x, own, k):
    s, _, n, f = own.shape
    return pl.pallas_call(functools.partial(join_body, k=k), out_shape=jax.ShapeDtypeStruct((2*s, 2, n, f), jnp.bfloat16),
        in_specs=[SMEM, VMEM, VMEM], out_specs=VMEM,
        compiler_params=pltpu.CompilerParams(vmem_limit_bytes=18<<20),
        cost_estimate=pl.CostEstimate(flops=10**7, bytes_accessed=7*10**6, transcendentals=0), name="whiten_join")(me, x, own)


def lag_basis(F, segs, parts):
    L = 2*F
    f = np.arange(F)[:,None]; t = np.arange(L)[None,:]
    ph = 2*np.pi/L*((f*t)%L)
    w = np.where(f==0,1.0,2.0)/(L*math.sqrt(segs))
    b = np.concatenate([w*np.cos(ph), -w*np.sin(ph)],0)
    hi = b.astype(np.float32).astype(ml_dtypes.bfloat16)
    lo = (b - hi.astype(np.float64)).astype(np.float32).astype(ml_dtypes.bfloat16)
    return jnp.asarray(np.concatenate([hi, hi, lo][:parts], 0))

def slot_codes(code_ref, owner_ref, me, cap):
    n = code_ref.shape[1]
    codes = [jnp.int32(-1)]*cap
    cnt = jnp.int32(0)
    for k in range(n):
        c = code_ref[0,k]
        mine = jnp.logical_and(c < CAND, owner_ref[0,k] == me)
        for s in range(cap):
            codes[s] = jnp.where(jnp.logical_and(mine, cnt == s), c, codes[s])
        cnt = cnt + mine.astype(jnp.int32)
    return codes

def plan_body(me_ref, code_ref, owner_ref, first_ref, second_ref, src_ref, codes_ref, *, cap, tile):
    codes = slot_codes(code_ref, owner_ref, me_ref[0], cap)
    for s in range(cap):
        codes_ref[s] = codes[s]
    S, _, n, _ = first_ref.shape
    row = lax.broadcasted_iota(jnp.int32, (cap*8, n), 0)
    col = lax.broadcasted_iota(jnp.int32, (cap*8, n), 1)
    target = jnp.zeros((cap*8, n), jnp.int32) - 1
    for s in range(cap):
        start = lax.rem(jnp.maximum(codes[s], 0), TILES)*tile
        i = row - s*8
        target = jnp.where((i >= 0) & (i < tile), start + i, target)
    hots = []
    for k in range(2):
        base = lax.rem(me_ref[0] + k, 2)*n
        hots.append(jnp.where(target == col + base, 1.0, 0.0).astype(jnp.bfloat16))
    for sg in range(S):
        picked = []
        for r in range(2):
            picked.append(sum(jnp.dot(hot, p[sg, r], preferred_element_type=jnp.float32)
                              for hot, p in zip(hots, (first_ref, second_ref))))
        sr, si = picked
        for q, v in enumerate((sr, sr + si, sr - si)):
            for s in range(cap):
                src_ref[s, sg*3+q] = v[s*8:(s+1)*8]


def plan(me, code, owner, first, second, cap, tile):
    S, _, _, F = first.shape
    return pl.pallas_call(functools.partial(plan_body, cap=cap, tile=tile),
        out_shape=[jax.ShapeDtypeStruct((cap, S*3, 8, F), jnp.float32), jax.ShapeDtypeStruct((cap,), jnp.int32)],
        in_specs=[SMEM]*3+[VMEM]*2, out_specs=[VMEM, SMEM],
        compiler_params=pltpu.CompilerParams(vmem_limit_bytes=18<<20),
        cost_estimate=pl.CostEstimate(flops=10**8, bytes_accessed=4*10**6, transcendentals=0), name="plan")(me, code, owner, first, second)


def stack_body(me_ref, codes_ref, src_ref, basis_ref, *refs, pieces, tile, cap, zero, C, has_prev):
    count = len(pieces)
    rec = refs[:count]
    out_ref, x_ref, stage, used, sem = refs[count + (1 if has_prev else 0):]
    F2 = basis_ref.shape[1]
    F = F2//2
    parts = basis_ref.shape[0]//F2
    used[0] = 0
    part = stage.shape[1]//tile

    def drain(b):
        for i in range(tile):
            pltpu.make_async_copy(stage.at[b, pl.ds(0, part)], out_ref.at[0, pl.ds(0, part)], sem.at[b, i]).wait()

    if zero:
        m = 160
        stage[0, :m] = jnp.zeros((m, F2), jnp.float32)
        @pl.loop(0, cap)
        def _(s):
            @pl.when(codes_ref[s] < 0)
            def _():
                copies = [pltpu.make_async_copy(stage.at[0, pl.ds(0, m)], out_ref.at[s, pl.ds(i*m, m)], sem.at[0, i]) for i in range(tile*C//m)]
                for cp in copies:
                    cp.start()
                for cp in copies:
                    cp.wait()

    for R, (one, two) in zip(rec, pieces):
        S, _, n, _ = R.shape
        off = jnp.where(me_ref[0] == 0, one[0], two[0])
        j0 = jnp.where(me_ref[0] == 0, one[1], two[1])*n
        @pl.loop(0, cap)
        def _(s, R=R, off=off, j0=j0, n=n, S=S):
            code = codes_ref[s]
            take = jnp.logical_and(code >= off*TILES, code < (off+1)*TILES)
            @pl.when(take)
            def _():
                @pl.loop(0, n//16)
                def _(g):
                    jj = pl.multiple_of(g*16, 16)
                    for ft in range(F//128):
                        fs = slice(ft*128, (ft+1)*128)
                        k1 = [jnp.zeros((16, 128), jnp.float32)]*tile
                        k2 = list(k1)
                        k3 = list(k1)
                        for sg in range(S):
                            rr = R[sg, 0, pl.ds(jj, 16), fs].astype(jnp.float32)
                            ri = R[sg, 1, pl.ds(jj, 16), fs].astype(jnp.float32)
                            both = rr + ri
                            q = sg*3
                            for i in range(tile):
                                k1[i] = k1[i] + src_ref[s, q, i:i+1, fs]*both
                                k2[i] = k2[i] + src_ref[s, q+1, i:i+1, fs]*rr
                                k3[i] = k3[i] + src_ref[s, q+2, i:i+1, fs]*ri
                        for i in range(tile):
                            for base, v in ((0, k1[i]-k3[i]), (F, k1[i]-k2[i])):
                                lo = base + ft*128
                                top = v.astype(jnp.bfloat16)
                                rows = pl.ds(pl.multiple_of(i*n + jj, 16), 16)
                                x_ref[rows, lo:lo+128] = top
                                if parts > 1:
                                    x_ref[rows, F2+lo:F2+lo+128] = (v - top.astype(jnp.float32)).astype(jnp.bfloat16)
                                if parts > 2:
                                    x_ref[rows, 2*F2+lo:2*F2+lo+128] = top
                b = lax.rem(used[0], 2)
                @pl.when(used[0] >= 2)
                def _():
                    drain(b)
                stage[b] = jnp.dot(x_ref[...], basis_ref[...], preferred_element_type=jnp.float32)
                for i in range(tile):
                    pltpu.make_async_copy(stage.at[b, pl.ds(i*n, n)], out_ref.at[s, pl.ds(pl.multiple_of(i*C + j0, 16), n)], sem.at[b, i]).start()
                used[0] = used[0] + 1

    for back in (1, 2):
        @pl.when(used[0] >= back)
        def _(back=back):
            drain(lax.rem(used[0] - back, 2))


def stack(me, codes, src, basis, pieces, recs, prev, C, tile, cap, zero=False):
    K, F2 = basis.shape
    rows = tile*recs[0].shape[2]
    hbm = pl.BlockSpec(memory_space=pl.ANY)
    args = [me, codes, src, basis] + recs
    specs = [SMEM, SMEM] + [VMEM]*(len(args)-2)
    alias = {}
    if prev is not None:
        alias = {len(args): 0}
        args.append(prev)
        specs.append(hbm)
    return pl.pallas_call(functools.partial(stack_body, pieces=pieces, tile=tile, cap=cap, zero=zero, C=C, has_prev=prev is not None),
        out_shape=jax.ShapeDtypeStruct((cap, tile*C, F2), jnp.float32),
        in_specs=specs, out_specs=hbm, input_output_aliases=alias,
        scratch_shapes=[pltpu.VMEM((rows, K), jnp.bfloat16), pltpu.VMEM((2, rows, F2), jnp.float32), pltpu.SMEM((1,), jnp.int32), pltpu.SemaphoreType.DMA((2, tile))],
        compiler_params=pltpu.CompilerParams(vmem_limit_bytes=18<<20),
        cost_estimate=pl.CostEstimate(flops=10**8, bytes_accessed=10**6, transcendentals=0), name="stack")(*args)


def on_device(spectra, pair_code, pair_owner):
    count = lax.axis_size("blk")
    hours = lax.axis_size("hour")
    me = lax.axis_index("hour").astype(jnp.int32).reshape(1)
    C, S, _, F = spectra.shape
    cap = pair_code.shape[1] // hours
    tile = C // TILES
    basis = lag_basis(F, S * hours, PARTS)

    def pull(v, zero, one):
        pairs = []
        for h, source in enumerate((zero, one)):
            for d in range(count):
                at = source(d)
                if at is not None:
                    pairs.append(((at % count) * hours + h, d * hours + h))
        return lax.ppermute(v, ("blk", "hour"), pairs)

    def swap(v):
        return lax.ppermute(v, "hour", [(h, hours - 1 - h) for h in range(hours)])

    def none(d):
        return None

    def x_of(d):
        return d % 4

    def y_ring(d):
        return (d // 16) * 16 + (d + 4) % 16 if x_of(d) == 0 else None

    def last_column(d):
        if x_of(d) != 3:
            return None
        return d + 13 if (d // 4) % 4 == 3 else d - 3

    def ahead(d):
        return d + 1 if x_of(d) != 3 else None

    peer = swap(spectra)
    own1, own2 = whiten_own(me, spectra)
    first = whiten_join(me, peer, own1, 0)
    near1 = pull(first, y_ring, none)
    got1 = pull(first, ahead, lambda d: d + 3)
    second = whiten_join(me, peer, own2, 1)
    near2 = pull(second, y_ring, none)
    wrap1 = pull(near1, last_column, none)
    got2 = pull(second, ahead, lambda d: d + 3)
    got1 = got1 + wrap1
    got3 = pull(got1, lambda d: d + 1, lambda d: d - 1)
    wrap2 = pull(near2, last_column, none)
    source, codes = plan(me, pair_code, pair_owner, first, second, cap, tile)
    swap1 = swap(got1)

    def add(prev, pieces, recs, zero=False):
        return stack(me, codes, source, basis, pieces, recs, prev, C, tile, cap, zero)

    out = add(None, (((0, 0), (0, 1)), ((0, 1), (0, 0)), ((1, 0), (3, 1))), [first, second, got1], True)
    got2, wrap2, out = lax.optimization_barrier((got2, wrap2, out))
    got2 = got2 + wrap2
    swap2 = swap(got2)
    swap3 = swap(got3)
    out = add(out, (((3, 1), (1, 0)), ((1, 1), (3, 0)), ((2, 0), (2, 1))), [swap1, got2, got3])
    out = add(out, (((3, 0), (1, 1)), ((2, 1), (2, 0))), [swap2, swap3])
    return out[None]


def solution(mesh):
    in_specs = (P("blk", "hour", None, None), P("blk", None), P("blk", None))
    out_specs = P("blk", "hour", None, None)
    return jax.shard_map(on_device, mesh=mesh, in_specs=in_specs, out_specs=out_specs, check_vma=False)
```
